256 devices in a mesh: pre: 8 (over z_hi, y), dec: 32 (over x, z_lo, core).
Axes of the slice: x: 4, y: 4, z: 8 (z_hi: 2, z_lo: 4; z = z_hi * 4 + z_lo), core: 2. Of those that a mesh axis runs over, the one named last changes fastest.
Arguments:
- prompt_x: bfloat16 [32768, 4096], P('dec', 'pre'), may hold values from -6 to 6
- w_dkv: bfloat16 [4096, 576], P('pre'), may hold values from -0.09375 to 0.09375
- kv_gain: float32 [512], replicated, may hold values from 0.25 to 1.75
- cache_pool: bfloat16 [1024, 36864], P('dec'), may hold values from -8 to 8
- queries: bfloat16 [256, 73728], P('dec', 'pre'), may hold values from -8 to 8
- row_lengths: int32 [256], P('dec'), may hold values from 1 to 256, as said below
- page_dest: int32 [512], replicated, may hold values from 0 to 31, as said below
- page_slot: int32 [512], replicated, may hold values from 0 to 31, as said below
- moe_x: bfloat16 [2048, 4096], P('dec'), may hold values from -6 to 6
- expert_ids: int32 [2048, 8], P('dec'), may hold values from 0 to 127, all different within a row; in each aligned block of 64 rows (0 to 63, 64 to 127, ...) at most 8 rows name the same one
- expert_weights: bfloat16 [2048, 8], P('dec'), may hold values from 0.099609375 to 1
- w_gate_up: bfloat16 [128, 2, 4096, 1024], P('dec', None, None, 'pre'), may hold values from -0.09375 to 0.09375
Outputs:
- attn_latent: bfloat16 [256, 65536], P('dec', 'pre')
- expert_hidden: bfloat16 [128, 256, 1024], P('dec', None, 'pre')
The draws below stay inside these ranges and needn't reach their ends.
Inputs may be any that keep to these rules, and one draw needn't show every extreme that they name: `row_lengths`: each decode row has at least one valid position; on every index of dec some row uses all 256 positions. `page_dest`: entry s * 16 + p names the dec index whose pool receives page p of the prompt held on dec index s. The 16 pages of one prompt go to 16 different indices, and one index receives a page of every prompt. `page_slot`: the page's row among the 32 rows of the receiving pool; no two pages that reach one index of dec share a row. `expert_ids`: each row names 8 different experts. In the rows of one index of dec (aligned blocks of 64 rows) no expert is named by more than 8 rows.
All inputs are finite; a program needn't handle non-finite values.
Results may differ from the reference program's by a relative error of at most 0.0059.
Values may be sent and summed in bfloat16 or wider, within the bound.
A program may use at most 128 MiB of HBM per device.

```python
import math
import jax
import jax.numpy as jnp
import numpy as np
from jax import lax

D = 4096
KVL = 512
LAT = 576
H = 128
HEAD_QK = 192
PAGE = 64
MI = 1024
EXP_DEV = 4
TOPK = 8
P_TOK = 1024
R_ATT = 8
PAGES_ROW = 4
R_MOE = 64
PP = 16
SLOTS = 32
EXPERTS = 128
CAP_E = 8
PROMPT_TOKENS = 32768
ROWS_MOE = 2048
N_DEC = 32


def page_tables(base_key):
    table_key = jax.random.fold_in(base_key, 5)
    crowded = jax.random.randint(jax.random.fold_in(table_key, 1), (), 0, N_DEC)
    sources = jnp.arange(N_DEC, dtype=jnp.int32)

    def one_source(source):
        source_key = jax.random.fold_in(table_key, 1000 + source)
        shuffled = jax.random.permutation(jax.random.fold_in(source_key, 1), N_DEC - 1)
        others = (crowded + 1 + shuffled[:PP - 1]) % N_DEC
        insert_at = jax.random.randint(jax.random.fold_in(source_key, 2), (), 0, PP)
        places = jnp.arange(PP, dtype=jnp.int32)
        before = jnp.take(others, jnp.clip(places, 0, PP - 2))
        shifted = jnp.take(others, jnp.clip(places - 1, 0, PP - 2))
        return jnp.where(places < insert_at, before, jnp.where(places == insert_at, crowded, shifted)).astype(jnp.int32)
    destinations = jax.vmap(one_source)(sources)

    def one_pool(target):
        return jax.random.permutation(jax.random.fold_in(table_key, 5000 + target), SLOTS).astype(jnp.int32)
    orders = jax.vmap(one_pool)(sources)
    slot_ids = orders[destinations, sources[:, None]]
    return (destinations.reshape(-1).astype(jnp.int32), slot_ids.reshape(-1).astype(jnp.int32))


def draw_page_dest(key, part):
    return page_tables(key)[0]


def draw_page_slot(key, part):
    return page_tables(key)[1]


def draw_row_lengths(key, part):
    key = jax.random.fold_in(key, 3)
    longest = PAGES_ROW * PAGE
    lengths_drawn = jax.random.randint(jax.random.fold_in(key, 1), (N_DEC, R_ATT), 1, longest + 1)
    chosen = jax.random.randint(jax.random.fold_in(key, 2), (N_DEC, 1), 0, R_ATT)
    full_row = jnp.arange(R_ATT, dtype=jnp.int32)[None, :] == chosen
    return jnp.where(full_row, longest, lengths_drawn).reshape(-1).astype(jnp.int32)


def draw_queries(key, part):
    key = jax.random.fold_in(key, 2)
    row_count = N_DEC * R_ATT
    query_shape = (row_count, H, LAT)
    values = jnp.clip(jax.random.normal(jax.random.fold_in(key, 1), query_shape, jnp.float32), -6.0, 6.0)
    return values.reshape(row_count, H * LAT).astype(jnp.bfloat16)


def draw_cache_pool(key, part):
    key = jax.random.fold_in(key, 4)
    pool_pages = SLOTS * N_DEC
    pool_shape = (pool_pages, PAGE, LAT)
    values = jnp.clip(jax.random.normal(jax.random.fold_in(key, 1), pool_shape, jnp.float32), -6.0, 6.0)
    return values.reshape(pool_pages, PAGE * LAT).astype(jnp.bfloat16)


def block_levels(key, extent, split, least, top_value):
    def one(dim, parts):
        draws = jax.random.uniform(jax.random.fold_in(jax.random.fold_in(key, 6), dim), (parts,), jnp.float32, least / len(split), top_value / len(split))
        return jnp.repeat(jnp.exp(draws), extent[dim] // parts).reshape((-1,) + (1,) * (len(extent) - dim - 1))

    gain = one(*split[0])
    for cut in split[1:]:
        gain = gain * one(*cut)
    return gain


def assign_block(rng, own, number, rows, count, top, bound, lean):
    order = jax.random.permutation(rng, count)
    heavy_load, common = portions_of(count, rows * top, bound, lean, True), portions_of(count, rows * top, bound, lean, False)
    places = jnp.arange(count)

    def named(lengths, rotation):
        used = int((lengths > 0).sum())
        fixed = max(1, used // 4)
        moved = fixed + (places - fixed + rotation * (used - fixed)) % max(1, count - fixed)
        return jnp.zeros((count,), jnp.int32).at[order[jnp.where(places < fixed, places, moved)]].set(jnp.asarray(lengths, jnp.int32))

    lengths = jnp.where(number % 4 == 0, named(heavy_load, number // 4), named(common, number - number // 4 - 1))
    mixed = jax.random.permutation(jax.random.fold_in(own, 3), count)
    giver, sink = mixed[0:count // 2 * 2:2], mixed[1:count // 2 * 2:2]
    room = jnp.minimum(lengths[giver] - 1, bound - lengths[sink]) // 2
    room = jnp.where((giver == order[0]) | (sink == order[0]) | (lengths[sink] == 0), 0, jnp.maximum(room, 0))
    moved = jax.random.randint(jax.random.fold_in(own, 4), (count // 2,), 0, 1 << 20) % (room + 1)
    lengths = lengths.at[giver].add(-moved).at[sink].add(moved)
    members = jnp.searchsorted(jnp.cumsum(lengths), jnp.arange(rows * top), side="right").astype(jnp.int32)
    table = members.reshape(top, rows).T
    table = table[jax.random.permutation(jax.random.fold_in(own, 1), rows)]
    rotation = jax.random.randint(jax.random.fold_in(own, 2), (rows, 1), 0, top)
    return jnp.take_along_axis(table, (jnp.arange(top)[None, :] + rotation) % top, axis=1)


def portions_of(number_of, total, reach, slope, full):
    portions = [(1 << 20) // math.isqrt(standing ** slope) + 1 for standing in range(1, number_of + 1)]
    largest = reach if full else min(reach, max(-(-total // number_of), total * portions[0] // sum(portions)))
    least = 1 if total - largest >= number_of - 1 else 0
    holding, rest = [largest] + [least] * (number_of - 1), total - largest - least * (number_of - 1)
    while rest > 0:
        free = [i for i in range(1, number_of) if holding[i] < largest] or [i for i in range(1, number_of) if holding[i] < reach]
        mass, budget = sum([portions[i] for i in free]), rest
        for i in free:
            more = min(reach - holding[i], max(1, budget * portions[i] // mass), rest)
            holding[i] = holding[i] + more
            rest = rest - more
    return np.array(holding)


def noise(rng, shape, scale, limit, cuts=(), kind=jnp.bfloat16):
    loudness = block_levels(rng, shape, cuts, -0.22, 0.18) if cuts else 1.0
    drawn = jax.random.normal(rng, shape, jnp.float32) * scale * loudness
    return jnp.minimum(jnp.maximum(drawn, -limit), limit).astype(kind)


def setup_inputs(seed: int = 0) -> dict:
    key_of = jax.random.split(jax.random.key(seed), 13)
    prompt_x = noise(key_of[0], (PROMPT_TOKENS, D), 1.0, 6.0, ((0, 32), (1, 8)))
    w_dkv = noise(key_of[1], (D, LAT), D ** -0.5, 0.09375, ((0, 8),))
    kv_gain = jnp.clip(1.0 + 0.15 * jax.random.normal(key_of[2], (KVL,), jnp.float32), 0.25, 1.75)
    cache_pool = draw_cache_pool(jax.random.fold_in(key_of[12], 71), 0)
    queries = draw_queries(jax.random.fold_in(key_of[12], 71), 0)
    row_lengths = draw_row_lengths(jax.random.fold_in(key_of[12], 71), 0)
    page_dest = draw_page_dest(jax.random.fold_in(key_of[12], 71), 0)
    page_slot = draw_page_slot(jax.random.fold_in(key_of[12], 71), 0)
    moe_x = noise(key_of[8], (ROWS_MOE, D), 1.0, 6.0, ((0, 32),))
    expert_ids_keys = jax.random.split(jax.random.fold_in(key_of[9], 1), ROWS_MOE // R_MOE)
    expert_ids_turns = jax.random.permutation(jax.random.fold_in(key_of[9], 3), ROWS_MOE // R_MOE)
    expert_ids = jax.vmap(lambda own, number: assign_block(jax.random.fold_in(key_of[9], 2), own, number, R_MOE, EXPERTS, TOPK, CAP_E, 2))(expert_ids_keys, expert_ids_turns).reshape((ROWS_MOE, TOPK))
    expert_weights = jnp.clip(0.099609375 + 0.9003906 * jax.random.uniform(key_of[10], (ROWS_MOE, TOPK), jnp.float32) ** block_levels(key_of[10], (ROWS_MOE, TOPK), ((0, 32),), -0.2, 0.2), 0.099609375, 1.0).astype(jnp.bfloat16)
    w_gate_up = noise(key_of[11], (EXPERTS, 2, D, MI), D ** -0.5, 0.09375, ((0, 32), (3, 8)))
    return {"prompt_x": prompt_x, "w_dkv": w_dkv, "kv_gain": kv_gain, "cache_pool": cache_pool, "queries": queries, "row_lengths": row_lengths, "page_dest": page_dest, "page_slot": page_slot, "moe_x": moe_x, "expert_ids": expert_ids, "expert_weights": expert_weights, "w_gate_up": w_gate_up}


NORM_EPSILON = 1e-06

def rotate_cache(latent, gain_vec, position):
    kv_count = gain_vec.shape[0]
    lat_part = latent[:, :kv_count]
    rope_part = latent[:, kv_count:]
    normed = lat_part * lax.rsqrt(lax.optimization_barrier(jnp.mean(lat_part * lat_part, axis=1, keepdims=True)) + NORM_EPSILON) * gain_vec
    halfway = rope_part.shape[1] // 2
    frequency = 10000.0 ** (-2.0 * jnp.arange(halfway, dtype=jnp.float32) / (2 * halfway))
    angles = position.astype(jnp.float32)[:, None] * frequency[None, :]
    lead_half = rope_part[:, :halfway]
    tail_half = rope_part[:, halfway:]
    cosine = jnp.cos(angles)
    sine_vals = jnp.sin(angles)
    rotated = jnp.concatenate([lead_half * cosine - tail_half * sine_vals, tail_half * cosine + lead_half * sine_vals], axis=1)
    return jnp.concatenate([normed, rotated], axis=1).astype(jnp.bfloat16)

def reference(prompt_x, w_dkv, kv_gain, cache_pool, queries, row_lengths, page_dest, page_slot, moe_x, expert_ids, expert_weights, w_gate_up):
    latent_raw = jnp.dot(prompt_x, w_dkv, preferred_element_type=jnp.float32)
    positions = jnp.tile(jnp.arange(P_TOK, dtype=jnp.int32), N_DEC)
    prompt_cache = rotate_cache(latent_raw, kv_gain, positions)
    page_rows = prompt_cache.reshape(N_DEC * PP, PAGE * LAT)
    target = (page_dest * SLOTS + page_slot).astype(jnp.int32)
    new_pool = cache_pool.at[target].set(page_rows)
    kv_rows = new_pool.reshape(N_DEC * R_ATT, PAGES_ROW * PAGE, LAT).astype(jnp.float32)
    query_view = queries.reshape(N_DEC * R_ATT, H, LAT).astype(jnp.float32)
    scores = jnp.einsum('rhc,rtc->rht', query_view, kv_rows, precision=lax.Precision.HIGHEST) * HEAD_QK ** (-0.5)
    in_length = jnp.arange(PAGES_ROW * PAGE, dtype=jnp.int32)[None, None, :] < row_lengths[:, None, None]
    masked = jnp.where(in_length, scores, -jnp.inf)
    top_score = lax.optimization_barrier(jnp.max(masked, axis=2, keepdims=True))
    weights_raw = jnp.exp(masked - top_score)
    attn_probs = (weights_raw / lax.optimization_barrier(jnp.sum(weights_raw, axis=2, keepdims=True))).astype(jnp.bfloat16)
    attn_sum = jnp.einsum('rht,rtc->rhc', attn_probs.astype(jnp.float32), kv_rows[:, :, :KVL], precision=lax.Precision.HIGHEST)
    attn_latent = attn_sum.astype(jnp.bfloat16).reshape(N_DEC * R_ATT, H * KVL)
    experts_all = EXP_DEV * N_DEC
    ids_view = expert_ids.reshape(N_DEC, R_MOE, TOPK)
    weight_view = expert_weights.reshape(N_DEC, R_MOE, TOPK).astype(jnp.float32)
    expert_axis = jnp.arange(experts_all, dtype=jnp.int32)
    matches = ids_view[:, :, :, None] == expert_axis[None, None, None, :]
    member = jnp.any(matches, axis=2)
    row_weight = lax.optimization_barrier(jnp.sum(jnp.where(matches, weight_view[:, :, :, None], 0.0), axis=2))
    member_int = member.astype(jnp.int32)
    row_rank = (jnp.cumsum(member_int, axis=1) - member_int).astype(jnp.int32)
    hit_slot = member[:, :, :, None] & (row_rank[:, :, :, None] == jnp.arange(CAP_E, dtype=jnp.int32)[None, None, None, :])
    slot_filled = jnp.any(hit_slot, axis=1)
    local_row = lax.optimization_barrier(jnp.sum(jnp.where(hit_slot, jnp.arange(R_MOE, dtype=jnp.int32)[None, :, None, None], 0), axis=1)).astype(jnp.int32)
    slot_row = (local_row + jnp.arange(N_DEC, dtype=jnp.int32)[:, None, None] * R_MOE).astype(jnp.int32)
    slot_weight = lax.optimization_barrier(jnp.sum(jnp.where(hit_slot, row_weight[:, :, :, None], 0.0), axis=1))

    def one_expert(expert):
        rows_index = lax.dynamic_index_in_dim(slot_row, expert, 1, keepdims=False).reshape(-1)
        filled = lax.dynamic_index_in_dim(slot_filled, expert, 1, keepdims=False).reshape(-1)
        weight = lax.dynamic_index_in_dim(slot_weight, expert, 1, keepdims=False).reshape(-1)
        gathered = jnp.where(filled[:, None], jnp.take(moe_x, rows_index, axis=0), 0).astype(jnp.bfloat16)
        expert_w = lax.dynamic_index_in_dim(w_gate_up, expert, 0, keepdims=False)
        gate_part = jnp.dot(gathered, expert_w[0], preferred_element_type=jnp.float32)
        upward = jnp.dot(gathered, expert_w[1], preferred_element_type=jnp.float32)
        return (jax.nn.silu(gate_part) * upward * weight[:, None]).astype(jnp.bfloat16)
    expert_hidden = lax.map(one_expert, expert_axis)
    return (attn_latent, expert_hidden)
```

```python
import jax
import jax.numpy as jnp
from jax import lax
from jax.experimental import pallas as pl
from jax.experimental.pallas import tpu as pltpu
from jax.sharding import PartitionSpec as P

KVL = 512
LAT = 576
HEAD_QK = 192
PAGE = 64
EXP_DEV = 4
P_TOK = 1024
R_ATT = 8
PAGES_ROW = 4
R_MOE = 64
PP = 16
SLOTS = 32
NORM_EPSILON = 1e-06

MESH = pl.DeviceIdType.MESH
A0, A1, B0, B1 = 0, 1, 2, 3
LEFT = [(-1, 0, A0), (-1, 0, A1), (-1, 0, B0), (-1, 0, B1), (2, 0, A0), (2, 0, B0), (-1, -1, B0), (-1, -1, B1),
        (-1, 1, B0), (-1, 1, B1), (-1, 2, B0), (-1, 2, B1), (2, -1, B0), (2, 1, B0), (2, 2, B0)]
RIGHT = [(1, 0, A1), (1, 0, A0), (1, 0, B1), (1, 0, B0), (2, 0, A1), (2, 0, B1), (1, -1, B1), (1, -1, B0),
         (1, 1, B1), (1, 1, B0), (1, 2, B1), (1, 2, B0), (2, -1, B1), (2, 1, B1), (2, 2, B1)]
BELOW = [(0, -1, B0), (0, -1, B1), (0, -1, A0), (0, -1, A1), (0, 2, B0), (0, 2, A0), (-1, -1, A0), (-1, -1, A1),
         (1, -1, A0), (1, -1, A1), (2, -1, A0), (2, -1, A1), (-1, 2, A0), (1, 2, A0), (2, 2, A0)]
ABOVE = [(0, 1, B1), (0, 1, B0), (0, 1, A1), (0, 1, A0), (0, 2, B1), (0, 2, A1), (-1, 1, A1), (-1, 1, A0),
         (1, 1, A1), (1, 1, A0), (2, 1, A1), (2, 1, A0), (-1, 2, A1), (1, 2, A1), (2, 2, A1)]
PASSES = {
    4: [[(0, 0), (-1, 0)]],
    5: [[(1, 0), (0, -1)]],
    6: [[(0, 1), (2, 0)]],
    8: [[(0, 2), (-1, -1)]],
    10: [[(1, -1), (-1, 1)]],
    11: [[(1, 1)]],
    13: [[(2, -1), (-1, 2)]],
    14: [[(2, 1), (1, 2)]],
    15: [[(2, 2)]],
}


def forwards(side, dx, dz, q):
    if side == "left":
        on = [(1, 0)] if dx == -1 and q in (A0, B0) else []
        return on + ([(0, 1), (0, -1)] if q in (A0, A1) else [])
    if side == "right":
        on = [(-1, 0)] if dx == 1 and q in (A1, B1) else []
        return on + ([(0, 1), (0, -1)] if q in (A0, A1) else [])
    if side == "below":
        on = [(0, 1)] if dz == -1 and q in (A0, B0) else []
        return on + ([(1, 0), (-1, 0)] if q in (B0, B1) else [])
    on = [(0, -1)] if dz == 1 and q in (A1, B1) else []
    return on + ([(1, 0), (-1, 0)] if q in (B0, B1) else [])


def device(x, y, z, c):
    return (lax.div(z, 4) * 4 + y, (x * 4 + lax.rem(z, 4)) * 2 + c)


def expert_kernel(moe_hbm, tag_ref, w_hbm, out_ref, rows, tags, wbuf, slot_ref, wt_ref,
                  load_sem, w_sem, ici_sem, pair_sem, recv_sem, recv2_sem, tag_send, tag_recv):
    pre, dec = lax.axis_index("pre"), lax.axis_index("dec")
    y = lax.rem(pre, 4)
    c = lax.rem(dec, 2)
    zl = lax.rem(lax.div(dec, 2), 4)
    x = lax.div(dec, 8)
    z = lax.div(pre, 4) * 4 + zl
    features = rows.shape[2]
    quarter = features // 4

    def chip(dx, dz):
        return lax.rem(x + dx + 4, 4) * 4 + lax.rem(z + dz + 8, 4)

    def peer(dx, dz, core):
        return device(lax.rem(x + dx + 4, 4), y, lax.rem(z + dz + 8, 8), core)

    loads = []
    for e in range(EXP_DEV):
        for t in range(2):
            load = pltpu.make_async_copy(w_hbm.at[e, t], wbuf.at[e, :, pl.ds(t * 128, 128)], w_sem.at[e * 2 + t])
            load.start()
            loads.append(load)
    own = pltpu.make_async_copy(moe_hbm, rows.at[dec], load_sem)
    own.start()
    tags[dec] = tag_ref[...]

    barrier = pltpu.get_barrier_semaphore()
    greeted = 0
    for dx in (0, 1, 2, 3):
        for dz in (-2, -1, 0, 1, 2):
            for dc in (0, 1):
                if (dx, dz, dc) != (0, 0, 0):
                    pl.semaphore_signal(barrier, inc=1, device_id=peer(dx, dz, lax.rem(c + dc, 2)), device_id_type=MESH)
                    greeted += 1
    pl.semaphore_wait(barrier, greeted)

    def piece(dx, dz, q, core):
        return rows.at[2 * chip(dx, dz) + core, :, pl.ds(q * quarter, quarter)]

    def push(dx, dz, q, sx, sz):
        pltpu.make_async_remote_copy(
            src_ref=piece(dx, dz, q, c), dst_ref=piece(dx, dz, q, c), send_sem=ici_sem,
            recv_sem=recv_sem.at[chip(dx, dz), q], device_id=peer(sx, sz, c), device_id_type=MESH).start()

    def share(dx, dz, q):
        pltpu.make_async_remote_copy(
            src_ref=piece(dx, dz, q, c), dst_ref=piece(dx, dz, q, c), send_sem=pair_sem,
            recv_sem=recv2_sem.at[chip(dx, dz), q], device_id=peer(0, 0, 1 - c), device_id_type=MESH).start()

    own.wait()
    for q in (A0, B0, A1, B1):
        push(0, 0, q, 1, 0)
        push(0, 0, (q + 2) % 4, 0, 1)
        push(0, 0, q ^ 1, -1, 0)
        push(0, 0, (q + 2) % 4 ^ 1, 0, -1)
    for q in range(4):
        share(0, 0, q)
    tag_copies = []
    for dx in (0, 1, 2, 3):
        for dz in (-1, 0, 1, 2):
            for dc in (0, 1):
                if (dx, dz, dc) != (0, 0, 0):
                    copy = pltpu.make_async_remote_copy(
                        src_ref=tag_ref, dst_ref=tags.at[dec], send_sem=tag_send.at[len(tag_copies)], recv_sem=tag_recv.at[dec],
                        device_id=peer(dx, dz, lax.rem(c + dc, 2)), device_id_type=MESH)
                    copy.start()
                    tag_copies.append(copy)

    def read_tags():
        for dx in (0, 1, 2, 3):
            for dz in (-1, 0, 1, 2):
                for dc in (0, 1):
                    if (dx, dz, dc) != (0, 0, 0):
                        s = 2 * chip(dx, dz) + lax.rem(c + dc, 2)
                        pltpu.make_async_copy(tags.at[s], tags.at[s], tag_recv.at[s]).wait()
        both = tags[...].astype(jnp.float32).reshape(16, 2, 16, 128)
        both = both[:, 0] + both[:, 1]
        ids, weights = both[:, :8], both[:, 8:]
        i0 = lax.broadcasted_iota(jnp.int32, (128, 128), 0)
        i1 = lax.broadcasted_iota(jnp.int32, (128, 128), 1)
        earlier = ((i0 < i1) & (lax.div(i0, 64) == lax.div(i1, 64))).astype(jnp.float32).astype(jnp.bfloat16)
        shift = jnp.where(lax.broadcasted_iota(jnp.int32, (16, 128), 1) >= 64, 8.0, 0.0)
        for e in range(EXP_DEV):
            hit = ids == (dec * EXP_DEV + e).astype(jnp.float32)
            member = jnp.sum(jnp.where(hit, 1.0, 0.0), axis=1)
            wt_ref[e] = jnp.sum(jnp.where(hit, weights, 0.0), axis=1)
            rank = jnp.dot(member.astype(jnp.bfloat16), earlier, preferred_element_type=jnp.float32)
            slot_ref[e] = jnp.where(member > 0.5, rank + shift, -1.0)

    def wait_item(dx, dz):
        for q in range(4):
            other = piece(dx, dz, q, 1 - c)
            pltpu.make_async_copy(other, other, recv2_sem.at[chip(dx, dz), q]).wait()

    def experts(items):
        blocks = [rows[pl.ds(2 * chip(dx, dz), 2)].reshape(128, features) for dx, dz in items]
        lhs = blocks[0] if len(blocks) == 1 else jnp.concatenate(blocks, axis=0)
        i0 = lax.broadcasted_iota(jnp.int32, (128, 128), 0)
        i1 = lax.broadcasted_iota(jnp.int32, (128, 128), 1)
        place = lax.broadcasted_iota(jnp.int32, (16, 128), 0).astype(jnp.float32)
        for e in range(EXP_DEV):
            both = jnp.dot(lhs, wbuf[e], preferred_element_type=jnp.float32)
            for n, (dx, dz) in enumerate(items):
                k = chip(dx, dz)
                gate, up = both[n * 128:(n + 1) * 128, :128], both[n * 128:(n + 1) * 128, 128:]
                wrow = wt_ref[e, pl.ds(k, 1), :]
                spread = jnp.where(i0 == i1, jnp.broadcast_to(wrow, (128, 128)), 0.0).astype(jnp.bfloat16)
                wcol = jnp.dot(spread, jnp.ones((128, 128), jnp.bfloat16), preferred_element_type=jnp.float32)
                hidden = (gate / (1.0 + jnp.exp(-gate)) * up * wcol).astype(jnp.bfloat16)
                srow = slot_ref[e, pl.ds(k, 1), :]
                choose = jnp.where(jnp.broadcast_to(srow, (16, 128)) == place, 1.0, 0.0).astype(jnp.bfloat16)
                out_ref[e, pl.ds(pl.multiple_of(k * 16, 16), 16), :] = jnp.dot(
                    choose, hidden, preferred_element_type=jnp.float32).astype(jnp.bfloat16)

    for n in range(1, 16):
        for side, plan in (("left", LEFT), ("right", RIGHT), ("below", BELOW), ("above", ABOVE)):
            dx, dz, q = plan[n - 1]
            got = piece(dx, dz, q, c)
            pltpu.make_async_copy(got, got, recv_sem.at[chip(dx, dz), q]).wait()
            for sx, sz in forwards(side, dx, dz, q):
                push(dx, dz, q, sx, sz)
            share(dx, dz, q)
        if n == 1:
            read_tags()
            for load in loads:
                load.wait()
        for items in PASSES.get(n, []):
            for dx, dz in items:
                wait_item(dx, dz)
            experts(items)

    sent = rows.at[pl.ds(0, 15)]
    pltpu.make_async_copy(sent, sent, ici_sem).wait()
    sent = rows.at[pl.ds(0, 16)]
    pltpu.make_async_copy(sent, sent, pair_sem).wait()
    for copy in tag_copies:
        copy.wait_send()


def expert_part(moe_x, expert_ids, expert_weights, w_gate_up):
    c = lax.rem(lax.axis_index("dec"), 2)
    tag = jnp.concatenate([expert_ids.T.astype(jnp.bfloat16), expert_weights.T], axis=0)
    zero = jnp.zeros_like(tag)
    tag = jnp.where(c == 0, jnp.concatenate([tag, zero], axis=1), jnp.concatenate([zero, tag], axis=1))
    features = moe_x.shape[1]
    return pl.pallas_call(
        expert_kernel,
        out_shape=jax.ShapeDtypeStruct((EXP_DEV, 256, 128), jnp.bfloat16),
        in_specs=[pl.BlockSpec(memory_space=pl.ANY), pl.BlockSpec(memory_space=pltpu.VMEM), pl.BlockSpec(memory_space=pl.ANY)],
        out_specs=pl.BlockSpec(memory_space=pltpu.VMEM),
        scratch_shapes=[
            pltpu.VMEM((32, R_MOE, features), jnp.bfloat16),
            pltpu.VMEM((32, 16, 128), jnp.bfloat16),
            pltpu.VMEM((EXP_DEV, features, 256), jnp.bfloat16),
            pltpu.VMEM((EXP_DEV, 16, 128), jnp.float32),
            pltpu.VMEM((EXP_DEV, 16, 128), jnp.float32),
            pltpu.SemaphoreType.DMA,
            pltpu.SemaphoreType.DMA((8,)),
            pltpu.SemaphoreType.DMA,
            pltpu.SemaphoreType.DMA,
            pltpu.SemaphoreType.DMA((16, 4)),
            pltpu.SemaphoreType.DMA((16, 4)),
            pltpu.SemaphoreType.DMA((31,)),
            pltpu.SemaphoreType.DMA((32,)),
        ],
        compiler_params=pltpu.CompilerParams(collective_id=0, has_side_effects=True, vmem_limit_bytes=56 * 1024 * 1024),
    )(moe_x, tag, w_gate_up)


def rotate_cache(latent, gain_vec, position):
    kv_count = gain_vec.shape[0]
    lat_part = latent[:, :kv_count]
    rope_part = latent[:, kv_count:]
    normed = (
        lat_part
        * lax.rsqrt(jnp.mean(lat_part * lat_part, axis=1, keepdims=True) + NORM_EPSILON)
        * gain_vec
    )
    halfway = rope_part.shape[1] // 2
    frequency = 10000.0 ** (-2.0 * jnp.arange(halfway, dtype=jnp.float32) / (2 * halfway))
    angles = position.astype(jnp.float32)[:, None] * frequency[None, :]
    lead_half = rope_part[:, :halfway]
    tail_half = rope_part[:, halfway:]
    cosine = jnp.cos(angles)
    sine_vals = jnp.sin(angles)
    rotated = jnp.concatenate(
        [lead_half * cosine - tail_half * sine_vals, tail_half * cosine + lead_half * sine_vals],
        axis=1,
    )
    return jnp.concatenate([normed, rotated], axis=1).astype(jnp.bfloat16)


def shards(
    prompt_x,
    w_dkv,
    kv_gain,
    cache_pool,
    queries,
    row_lengths,
    page_dest,
    page_slot,
    moe_x,
    expert_ids,
    expert_weights,
    w_gate_up,
):
    n_dec = lax.axis_size("dec")
    dec_index = lax.axis_index("dec")
    dest_table = page_dest.reshape(n_dec, PP)
    slot_table = page_slot.reshape(n_dec, PP)
    my_dest = lax.dynamic_index_in_dim(dest_table, dec_index, 0, keepdims=False)
    select = (my_dest[None, :] == jnp.arange(n_dec, dtype=jnp.int32)[:, None]).astype(jnp.bfloat16)
    partial_sum = jnp.dot(prompt_x, w_dkv, preferred_element_type=jnp.float32)
    latent_total = lax.psum(partial_sum, "pre")
    positions = jnp.arange(P_TOK, dtype=jnp.int32)
    prompt_cache = rotate_cache(latent_total, kv_gain, positions)
    page_rows = prompt_cache.reshape(PP, PAGE * LAT)
    outgoing = jnp.dot(select, page_rows, preferred_element_type=jnp.float32).astype(jnp.bfloat16)
    arrived = lax.all_to_all(outgoing, "dec", split_axis=0, concat_axis=0, tiled=True)
    hit_page = dest_table == dec_index
    from_source = jnp.any(hit_page, axis=1)
    source_slot = jnp.sum(jnp.where(hit_page, slot_table, 0), axis=1)
    placing = (source_slot[None, :] == jnp.arange(SLOTS, dtype=jnp.int32)[:, None]) & from_source[
        None, :
    ]
    landed = jnp.dot(
        placing.astype(jnp.bfloat16), arrived, preferred_element_type=jnp.float32
    ).astype(jnp.bfloat16)
    new_pool = jnp.where(jnp.any(placing, axis=1)[:, None], landed, cache_pool)
    kv_rows = new_pool.reshape(R_ATT, PAGES_ROW * PAGE, LAT)
    heads_here = queries.shape[1] // LAT
    query_view = queries.reshape(R_ATT, heads_here, LAT)
    scores = jnp.einsum(
        "rhc,rtc->rht", query_view, kv_rows, preferred_element_type=jnp.float32
    ) * HEAD_QK ** (-0.5)
    in_length = (
        jnp.arange(PAGES_ROW * PAGE, dtype=jnp.int32)[None, None, :] < row_lengths[:, None, None]
    )
    masked = jnp.where(in_length, scores, -jnp.inf)
    top_score = jnp.max(masked, axis=2, keepdims=True)
    weights_raw = jnp.exp(masked - top_score)
    attn_probs = (weights_raw / jnp.sum(weights_raw, axis=2, keepdims=True)).astype(jnp.bfloat16)
    attn_sum = jnp.einsum(
        "rht,rtc->rhc", attn_probs, kv_rows[:, :, :KVL], preferred_element_type=jnp.float32
    )
    attn_latent = attn_sum.astype(jnp.bfloat16).reshape(R_ATT, heads_here * KVL)
    expert_hidden = expert_part(moe_x, expert_ids, expert_weights, w_gate_up)
    return (attn_latent, expert_hidden)


def solution(mesh):
    return jax.shard_map(
        shards,
        mesh=mesh,
        in_specs=(
            P("dec", "pre"),
            P("pre", None),
            P(),
            P("dec", None),
            P("dec", "pre"),
            P("dec"),
            P(),
            P(),
            P("dec", None),
            P("dec", None),
            P("dec", None),
            P("dec", None, None, "pre"),
        ),
        out_specs=(P("dec", "pre"), P("dec", None, "pre")),
        check_vma=False,
    )
```

```python
import jax
import jax.numpy as jnp
import numpy as np
from jax import lax
from jax.experimental import pallas as pl
from jax.experimental.pallas import tpu as pltpu
from jax.sharding import PartitionSpec as P

KVL = 512
LAT = 576
HEAD_QK = 192
PAGE = 64
EXP_DEV = 4
P_TOK = 1024
R_ATT = 8
PAGES_ROW = 4
R_MOE = 64
PP = 16
SLOTS = 32
NORM_EPSILON = 1e-06

MESH = pl.DeviceIdType.MESH
A0, A1, B0, B1 = 0, 1, 2, 3
LEFT = [(-1, 0, A0), (-1, 0, A1), (-1, 0, B0), (-1, 0, B1), (2, 0, A0), (2, 0, B0), (-1, -1, B0), (-1, -1, B1),
        (-1, 1, B0), (-1, 1, B1), (-1, 2, B0), (-1, 2, B1), (2, -1, B0), (2, 1, B0), (2, 2, B0)]
RIGHT = [(1, 0, A1), (1, 0, A0), (1, 0, B1), (1, 0, B0), (2, 0, A1), (2, 0, B1), (1, -1, B1), (1, -1, B0),
         (1, 1, B1), (1, 1, B0), (1, 2, B1), (1, 2, B0), (2, -1, B1), (2, 1, B1), (2, 2, B1)]
BELOW = [(0, -1, B0), (0, -1, B1), (0, -1, A0), (0, -1, A1), (0, 2, B0), (0, 2, A0), (-1, -1, A0), (-1, -1, A1),
         (1, -1, A0), (1, -1, A1), (2, -1, A0), (2, -1, A1), (-1, 2, A0), (1, 2, A0), (2, 2, A0)]
ABOVE = [(0, 1, B1), (0, 1, B0), (0, 1, A1), (0, 1, A0), (0, 2, B1), (0, 2, A1), (-1, 1, A1), (-1, 1, A0),
         (1, 1, A1), (1, 1, A0), (2, 1, A1), (2, 1, A0), (-1, 2, A1), (1, 2, A1), (2, 2, A1)]
def forwards(side, dx, dz, q):
    if side == "left":
        on = [(1, 0)] if dx == -1 and q in (A0, B0) else []
        return on + ([(0, 1), (0, -1)] if q in (A0, A1) else [])
    if side == "right":
        on = [(-1, 0)] if dx == 1 and q in (A1, B1) else []
        return on + ([(0, 1), (0, -1)] if q in (A0, A1) else [])
    if side == "below":
        on = [(0, 1)] if dz == -1 and q in (A0, B0) else []
        return on + ([(1, 0), (-1, 0)] if q in (B0, B1) else [])
    on = [(0, -1)] if dz == 1 and q in (A1, B1) else []
    return on + ([(1, 0), (-1, 0)] if q in (B0, B1) else [])


def device(x, y, z, c):
    return (lax.div(z, 4) * 4 + y, (x * 4 + lax.rem(z, 4)) * 2 + c)


HALVES = 2
HPAGES = PP // HALVES
NEAR = (0, 1, -1, 2)
PASSES = {
    2: [(0, 0)],
    4: [(-1, 0)],
    5: [(1, 0), (0, -1)],
    6: [(0, 1), (2, 0)],
    7: [(0, 2)],
    8: [(-1, -1)],
    10: [(1, -1), (-1, 1), (1, 1)],
    13: [(2, -1), (-1, 2)],
    14: [(2, 1), (1, 2)],
    15: [(2, 2)],
}


def main_kernel(px_hbm, wd_ref, gain_ref, rope_hbm, pool_ref, q_ref, len_ref, dest_ref, slot_in_ref, moe_hbm, tag_ref, w_hbm,
                att_ref, out_ref,
                px, rope, rs_send, rs_recv, acc, zx_send, zx_recv, cache, pg_send, pg_recv, kv_send, kv_recv, kvbuf, q_recv, o_send,
                page_of, slot_of, src_of, rows, tags, wbuf, slot_ref, wt_ref,
                px_sem, rope_sem, rs_ssem, rs_rsem, zx_ssem, zx_rsem, pg_ssem, pg_rsem, kv_ssem, kv_rsem, q_ssem, q_rsem, o_ssem, o_rsem,
                load_sem, w_sem, ici_sem, pair_sem, recv_sem, recv2_sem, tag_send, tag_recv):
    pre, dec = lax.axis_index("pre"), lax.axis_index("dec")
    y = lax.rem(pre, 4)
    c = lax.rem(dec, 2)
    zl = lax.rem(lax.div(dec, 2), 4)
    x = lax.div(dec, 8)
    z = lax.div(pre, 4) * 4 + zl
    features = rows.shape[2]
    quarter = features // 4

    def chip(dx, dz):
        return lax.rem(x + dx + 4, 4) * 4 + lax.rem(z + dz + 8, 4)

    def peer(dx, dz, core):
        return device(lax.rem(x + dx + 4, 4), y, lax.rem(z + dz + 8, 8), core)

    def ypeer(dy):
        return device(x, lax.rem(y + dy, 4), z, c)

    def remote(src, dst, ssem, rsem, where):
        copy = pltpu.make_async_remote_copy(
            src_ref=src, dst_ref=dst, send_sem=ssem, recv_sem=rsem, device_id=where, device_id_type=MESH)
        copy.start()
        return copy

    def landed(ref, sem):
        pltpu.make_async_copy(ref, ref, sem).wait()

    own = pltpu.make_async_copy(moe_hbm, rows.at[chip(0, 0), pl.ds(pl.multiple_of(c * R_MOE, R_MOE), R_MOE)], load_sem)
    own.start()
    px_load = pltpu.make_async_copy(px_hbm, px, px_sem)
    px_load.start()
    rope_load = pltpu.make_async_copy(rope_hbm.at[:, y], rope, rope_sem)
    rope_load.start()
    loads = []
    for e in range(EXP_DEV):
        for t in range(2):
            load = pltpu.make_async_copy(w_hbm.at[e, t], wbuf.at[:, pl.ds((e * 2 + t) * 128, 128)], w_sem.at[e * 2 + t])
            load.start()
            loads.append(load)
    tags[dec] = tag_ref[...]

    barrier = pltpu.get_barrier_semaphore()
    greeted = 0
    for dx in (0, 1, 2, 3):
        for dz in (-2, -1, 0, 1, 2):
            for dc in (0, 1):
                if (dx, dz, dc) != (0, 0, 0):
                    pl.semaphore_signal(barrier, inc=1, device_id=peer(dx, dz, lax.rem(c + dc, 2)), device_id_type=MESH)
                    greeted += 1
    for dy in (1, 2, 3):
        pl.semaphore_signal(barrier, inc=1, device_id=ypeer(dy), device_id_type=MESH)
        greeted += 1
    pl.semaphore_signal(barrier, inc=1, device_id=peer(0, 4, c), device_id_type=MESH)
    greeted += 1
    pl.semaphore_wait(barrier, greeted)

    def piece(dx, dz, q, core):
        return rows.at[chip(dx, dz), pl.ds(pl.multiple_of(core * R_MOE, R_MOE), R_MOE), pl.ds(q * quarter, quarter)]

    def push(dx, dz, q, sx, sz):
        remote(piece(dx, dz, q, c), piece(dx, dz, q, c), ici_sem, recv_sem.at[chip(dx, dz), q], peer(sx, sz, c))

    def share(dx, dz, q):
        remote(piece(dx, dz, q, c), piece(dx, dz, q, c), pair_sem, recv2_sem.at[chip(dx, dz), q], peer(0, 0, 1 - c))

    own.wait()
    for q in (A0, B0, A1, B1):
        push(0, 0, q, 1, 0)
        push(0, 0, (q + 2) % 4, 0, 1)
        push(0, 0, q ^ 1, -1, 0)
        push(0, 0, (q + 2) % 4 ^ 1, 0, -1)

    px_load.wait()
    rs_copies = []
    for h in range(HALVES):
        for dy in (2, 1, 3, 0):
            yy = lax.rem(y + dy, 4)
            lhs = px[pl.ds(h * HPAGES, HPAGES), yy].reshape(HPAGES * 16, px.shape[3])
            part = jnp.dot(lhs, wd_ref[...], preferred_element_type=jnp.float32)
            if dy:
                rs_send[dy - 1, h] = part.astype(jnp.bfloat16)
                rs_copies.append(remote(rs_send.at[dy - 1, h], rs_recv.at[dy - 1, h], rs_ssem.at[dy - 1, h], rs_rsem.at[dy - 1, h], ypeer(dy)))
            else:
                acc[h] = part

    for q in range(4):
        share(0, 0, q)
    tag_copies = []
    for dx in (0, 1, 2, 3):
        for dz in NEAR:
            for dc in (0, 1):
                if (dx, dz, dc) != (0, 0, 0):
                    n = len(tag_copies)
                    tag_copies.append(remote(tag_ref, tags.at[dec], tag_send.at[n], tag_recv.at[dec], peer(dx, dz, lax.rem(c + dc, 2))))
    q_copies = []
    for dy in (1, 2, 3):
        yy = lax.rem(y + dy, 4)
        q_copies.append(remote(q_ref.at[yy], q_recv.at[y], q_ssem.at[dy - 1], q_rsem.at[y], ypeer(dy)))
    q_recv[y] = q_ref[y]

    dests = [dest_ref[dec * PP + p] for p in range(PP)]

    def find_page(d, carry):
        found = jnp.int32(0)
        for p in range(PP):
            found = jnp.where(dests[p] == d, p, found)
        page_of[d] = found
        return carry

    lax.fori_loop(0, 32, find_page, 0)

    def find_slot(s, carry):
        found = jnp.int32(-1)
        for p in range(PP):
            found = jnp.where(dest_ref[s * PP + p] == dec, slot_in_ref[s * PP + p], found)
        slot_of[s] = found
        return carry

    lax.fori_loop(0, 32, find_slot, 0)

    def find_source(k, carry):
        found = jnp.int32(-1)
        for s in range(32):
            found = jnp.where(slot_of[s] == k, s, found)
        src_of[k] = found
        return carry

    lax.fori_loop(0, SLOTS, find_source, 0)

    def read_tags():
        for dx in (0, 1, 2, 3):
            for dz in NEAR:
                for dc in (0, 1):
                    if (dx, dz, dc) != (0, 0, 0):
                        s = 2 * chip(dx, dz) + lax.rem(c + dc, 2)
                        landed(tags.at[s], tag_recv.at[s])
        both = tags[...].astype(jnp.float32).reshape(16, 2, 16, 128)
        both = both[:, 0] + both[:, 1]
        ids, weights = both[:, :8], both[:, 8:]
        i0 = lax.broadcasted_iota(jnp.int32, (128, 128), 0)
        i1 = lax.broadcasted_iota(jnp.int32, (128, 128), 1)
        earlier = ((i0 < i1) & (lax.div(i0, 64) == lax.div(i1, 64))).astype(jnp.float32).astype(jnp.bfloat16)
        shift = jnp.where(lax.broadcasted_iota(jnp.int32, (16, 128), 1) >= 64, 8.0, 0.0)
        for e in range(EXP_DEV):
            hit = ids == (dec * EXP_DEV + e).astype(jnp.float32)
            member = jnp.sum(jnp.where(hit, 1.0, 0.0), axis=1)
            wt_ref[e] = jnp.sum(jnp.where(hit, weights, 0.0), axis=1)
            rank = jnp.dot(member.astype(jnp.bfloat16), earlier, preferred_element_type=jnp.float32)
            slot_ref[e] = jnp.where(member > 0.5, rank + shift, -1.0)

    def wait_item(dx, dz):
        for q in range(4):
            landed(piece(dx, dz, q, 1 - c), recv2_sem.at[chip(dx, dz), q])

    def experts(dx, dz):
        k = chip(dx, dz)
        i0 = lax.broadcasted_iota(jnp.int32, (128, 128), 0)
        i1 = lax.broadcasted_iota(jnp.int32, (128, 128), 1)
        place = lax.broadcasted_iota(jnp.int32, (16, 128), 0).astype(jnp.float32)
        both = jnp.dot(rows[k], wbuf[...], preferred_element_type=jnp.float32)
        for e in range(EXP_DEV):
            gate, up = both[:, e * 256:e * 256 + 128], both[:, e * 256 + 128:e * 256 + 256]
            wrow = wt_ref[e, pl.ds(k, 1), :]
            spread = jnp.where(i0 == i1, jnp.broadcast_to(wrow, (128, 128)), 0.0).astype(jnp.bfloat16)
            wcol = jnp.dot(spread, jnp.ones((128, 128), jnp.bfloat16), preferred_element_type=jnp.float32)
            hidden = (gate / (1.0 + jnp.exp(-gate)) * up * wcol).astype(jnp.bfloat16)
            srow = slot_ref[e, pl.ds(k, 1), :]
            choose = jnp.where(jnp.broadcast_to(srow, (16, 128)) == place, 1.0, 0.0).astype(jnp.bfloat16)
            out_ref[e, pl.ds(pl.multiple_of(k * 16, 16), 16), :] = jnp.dot(
                choose, hidden, preferred_element_type=jnp.float32).astype(jnp.bfloat16)

    zx_copies, pg_copies, kv_copies, o_copies = [], [], [], []

    def add_y(h):
        total = acc[h]
        for dy in (1, 2, 3):
            landed(rs_recv.at[dy - 1, h], rs_rsem.at[dy - 1, h])
            total = total + rs_recv[dy - 1, h].astype(jnp.float32)
        acc[h] = total
        zx_send[h] = total.astype(jnp.bfloat16)
        zx_copies.append(remote(zx_send.at[h], zx_recv.at[h], zx_ssem.at[h], zx_rsem.at[h], peer(0, 4, c)))

    def finish_cache(h):
        landed(zx_recv.at[h], zx_rsem.at[h])
        if h == 0:
            rope_load.wait()
        total = acc[h] + zx_recv[h].astype(jnp.float32)
        lat, turn = total[:, :KVL], total[:, KVL:]
        normed = lat * lax.rsqrt(jnp.mean(lat * lat, axis=1, keepdims=True) + NORM_EPSILON) * gain_ref[...]
        table = rope[pl.ds(h * HPAGES, HPAGES)].reshape(HPAGES * 16, 128)
        swapped = jnp.concatenate([turn[:, 32:], turn[:, :32]], axis=1)
        turned = turn * table[:, :64] + swapped * table[:, 64:]
        done = jnp.concatenate([normed, turned], axis=1).astype(jnp.bfloat16)
        cache[pl.ds(h * HPAGES, HPAGES)] = done.reshape(HPAGES, 16, LAT)

    def send_pages():
        n = 0
        for dx in (0, 1, 2, 3):
            for dz in NEAR:
                for dc in (0, 1):
                    cc = lax.rem(c + dc, 2)
                    page = cache[page_of[2 * chip(dx, dz) + cc]]
                    if (dx, dz, dc) == (0, 0, 0):
                        pg_recv[dec] = page
                        continue
                    pg_send[n] = page
                    pg_copies.append(remote(pg_send.at[n], pg_recv.at[dec], pg_ssem.at[n], pg_rsem.at[dec], peer(dx, dz, cc)))
                    n += 1

    def place_pages():
        for dx in (0, 1, 2, 3):
            for dz in NEAR:
                for dc in (0, 1):
                    if (dx, dz, dc) != (0, 0, 0):
                        s = 2 * chip(dx, dz) + lax.rem(c + dc, 2)
                        landed(pg_recv.at[s], pg_rsem.at[s])
        for k in range(SLOTS):
            kv_send[k // 8, k % 8] = pg_recv[jnp.maximum(src_of[k], 0)]
        for dy in (1, 2, 3):
            yy = lax.rem(y + dy, 4)
            kv_copies.append(remote(kv_send.at[yy], kv_recv.at[y], kv_ssem.at[dy - 1], kv_rsem.at[y], ypeer(dy)))
        kv_recv[y] = kv_send[y]

    def attend():
        for dy in (1, 2, 3):
            yy = lax.rem(y + dy, 4)
            landed(kv_recv.at[yy], kv_rsem.at[yy])
            landed(q_recv.at[yy], q_rsem.at[yy])
        for k in range(8):
            fresh = src_of[y * 8 + k] >= 0
            for yy in range(4):
                kvbuf[k // 4, yy, k % 4] = jnp.where(fresh, kv_recv[yy, k], pool_ref[k, yy])
        col = lax.broadcasted_iota(jnp.int32, (64, 256), 1)
        at = lax.rem(lax.div(col, 16), 4) * PAGE + lax.div(col, 64) * 16 + lax.rem(col, 16)
        for rr in range(2):
            kv = kvbuf[rr].reshape(PAGES_ROW * PAGE, LAT)
            query = q_recv[:, rr].reshape(64, LAT)
            scores = lax.dot_general(query, kv, (((1,), (1,)), ((), ())), preferred_element_type=jnp.float32) * HEAD_QK ** (-0.5)
            masked = jnp.where(at < len_ref[2 * y + rr], scores, -jnp.inf)
            raw = jnp.exp(masked - jnp.max(masked, axis=1, keepdims=True))
            probs = (raw / jnp.sum(raw, axis=1, keepdims=True)).astype(jnp.bfloat16)
            got = jnp.dot(probs, kv[:, :KVL], preferred_element_type=jnp.float32).astype(jnp.bfloat16)
            o_send[:, rr] = got.reshape(4, 16, KVL)
        for dy in (1, 2, 3):
            yy = lax.rem(y + dy, 4)
            o_copies.append(remote(o_send.at[yy], att_ref.at[y], o_ssem.at[dy - 1], o_rsem.at[y], ypeer(dy)))
        att_ref[y] = o_send[y]

    events = {3: [lambda: add_y(0)], 5: [lambda: add_y(1)], 6: [lambda: finish_cache(0)],
              8: [lambda: finish_cache(1), send_pages], 11: [place_pages], 13: [attend]}

    for n in range(1, 16):
        for side, plan in (("left", LEFT), ("right", RIGHT), ("below", BELOW), ("above", ABOVE)):
            dx, dz, q = plan[n - 1]
            landed(piece(dx, dz, q, c), recv_sem.at[chip(dx, dz), q])
            for sx, sz in forwards(side, dx, dz, q):
                push(dx, dz, q, sx, sz)
            share(dx, dz, q)
        if n == 2:
            read_tags()
            for load in loads:
                load.wait()
        for event in events.get(n, []):
            event()
        for dx, dz in PASSES.get(n, []):
            wait_item(dx, dz)
            experts(dx, dz)

    for dy in (1, 2, 3):
        yy = lax.rem(y + dy, 4)
        landed(att_ref.at[yy], o_rsem.at[yy])
    landed(rows.at[pl.ds(0, 8)], pair_sem)
    landed(rows.at[pl.ds(0, 15), pl.ds(0, R_MOE)], ici_sem)
    for copy in tag_copies + q_copies + rs_copies + zx_copies + pg_copies + kv_copies + o_copies:
        copy.wait_send()


def rope_table():
    place = np.arange(P_TOK, dtype=np.float32)[:, None]
    angle = (place * (10000.0 ** (-2.0 * np.arange(32, dtype=np.float64) / 64)).astype(np.float32)[None, :]).astype(np.float64)
    cosine, sine = np.cos(angle), np.sin(angle)
    return np.concatenate([cosine, cosine, -sine, sine], axis=1).astype(np.float32)


def shards(
    prompt_x,
    w_dkv,
    kv_gain,
    cache_pool,
    queries,
    row_lengths,
    page_dest,
    page_slot,
    moe_x,
    expert_ids,
    expert_weights,
    w_gate_up,
):
    dec = lax.axis_index("dec")
    y = lax.rem(lax.axis_index("pre"), 4)
    c = lax.rem(dec, 2)
    tag = jnp.concatenate([expert_ids.T.astype(jnp.bfloat16), expert_weights.T], axis=0)
    zero = jnp.zeros_like(tag)
    tag = jnp.where(c == 0, jnp.concatenate([tag, zero], axis=1), jnp.concatenate([zero, tag], axis=1))
    features = moe_x.shape[1]
    part = prompt_x.shape[1]
    px = prompt_x.reshape(PP, 4, 16, part)
    rope = jnp.asarray(rope_table()).reshape(PP, 4, 16, 128)
    pool = lax.dynamic_slice_in_dim(cache_pool, y * 8, 8, 0).reshape(8, 4, 16, LAT)
    heads = queries.shape[1] // LAT
    q = queries.reshape(4, 2, heads, LAT)
    vmem = pl.BlockSpec(memory_space=pltpu.VMEM)
    smem = pl.BlockSpec(memory_space=pltpu.SMEM)
    hbm = pl.BlockSpec(memory_space=pl.ANY)
    dma = pltpu.SemaphoreType.DMA
    bf = jnp.bfloat16
    att, out = pl.pallas_call(
        main_kernel,
        out_shape=(jax.ShapeDtypeStruct((4, 2, heads, KVL), bf), jax.ShapeDtypeStruct((EXP_DEV, 256, 128), bf)),
        in_specs=[hbm, vmem, vmem, hbm, vmem, vmem, smem, smem, smem, hbm, vmem, hbm],
        out_specs=(vmem, vmem),
        scratch_shapes=[
            pltpu.VMEM((PP, 4, 16, part), bf),
            pltpu.VMEM((PP, 16, 128), jnp.float32),
            pltpu.VMEM((3, HALVES, HPAGES * 16, LAT), bf),
            pltpu.VMEM((3, HALVES, HPAGES * 16, LAT), bf),
            pltpu.VMEM((HALVES, HPAGES * 16, LAT), jnp.float32),
            pltpu.VMEM((HALVES, HPAGES * 16, LAT), bf),
            pltpu.VMEM((HALVES, HPAGES * 16, LAT), bf),
            pltpu.VMEM((PP, 16, LAT), bf),
            pltpu.VMEM((31, 16, LAT), bf),
            pltpu.VMEM((32, 16, LAT), bf),
            pltpu.VMEM((4, 8, 16, LAT), bf),
            pltpu.VMEM((4, 8, 16, LAT), bf),
            pltpu.VMEM((2, 4, 4, 16, LAT), bf),
            pltpu.VMEM((4, 2, heads, LAT), bf),
            pltpu.VMEM((4, 2, heads, KVL), bf),
            pltpu.SMEM((32,), jnp.int32),
            pltpu.SMEM((32,), jnp.int32),
            pltpu.SMEM((32,), jnp.int32),
            pltpu.VMEM((16, 2 * R_MOE, features), bf),
            pltpu.VMEM((32, 16, 128), bf),
            pltpu.VMEM((features, EXP_DEV * 256), bf),
            pltpu.VMEM((EXP_DEV, 16, 128), jnp.float32),
            pltpu.VMEM((EXP_DEV, 16, 128), jnp.float32),
            dma, dma, dma((3, HALVES)), dma((3, HALVES)), dma((HALVES,)), dma((HALVES,)), dma((31,)), dma((32,)),
            dma((3,)), dma((4,)), dma((3,)), dma((4,)), dma((3,)), dma((4,)),
            dma, dma((8,)), dma, dma, dma((16, 4)), dma((16, 4)), dma((31,)), dma((32,)),
        ],
        compiler_params=pltpu.CompilerParams(collective_id=0, has_side_effects=True, vmem_limit_bytes=58 * 1024 * 1024),
    )(px, w_dkv, kv_gain.reshape(1, KVL), rope, pool, q, row_lengths, page_dest, page_slot, moe_x, tag, w_gate_up)
    return (att.reshape(R_ATT, heads * KVL), out)


def solution(mesh):
    return jax.shard_map(
        shards,
        mesh=mesh,
        in_specs=(
            P("dec", "pre"),
            P("pre", None),
            P(),
            P("dec", None),
            P("dec", "pre"),
            P("dec"),
            P(),
            P(),
            P("dec", None),
            P("dec", None),
            P("dec", None),
            P("dec", None, None, "pre"),
        ),
        out_specs=(P("dec", "pre"), P("dec", None, "pre")),
        check_vma=False,
    )
```

```python
import jax
import jax.numpy as jnp
import numpy as np
from jax import lax
from jax.experimental import pallas as pl
from jax.experimental.pallas import tpu as pltpu
from jax.sharding import PartitionSpec as P

KVL = 512
LAT = 576
HEAD_QK = 192
PAGE = 64
EXP_DEV = 4
P_TOK = 1024
R_ATT = 8
PAGES_ROW = 4
R_MOE = 64
PP = 16
SLOTS = 32
NORM_EPSILON = 1e-06

MESH = pl.DeviceIdType.MESH
A0, A1, B0, B1 = 0, 1, 2, 3
LEFT = [(-1, 0, A0), (-1, 0, A1), (-1, 0, B0), (-1, 0, B1), (2, 0, A0), (2, 0, B0), (-1, -1, B0), (-1, -1, B1),
        (-1, 1, B0), (-1, 1, B1), (-1, 2, B0), (-1, 2, B1), (2, -1, B0), (2, 1, B0), (2, 2, B0)]
RIGHT = [(1, 0, A1), (1, 0, A0), (1, 0, B1), (1, 0, B0), (2, 0, A1), (2, 0, B1), (1, -1, B1), (1, -1, B0),
         (1, 1, B1), (1, 1, B0), (1, 2, B1), (1, 2, B0), (2, -1, B1), (2, 1, B1), (2, 2, B1)]
BELOW = [(0, -1, B0), (0, -1, B1), (0, -1, A0), (0, -1, A1), (0, 2, B0), (0, 2, A0), (-1, -1, A0), (-1, -1, A1),
         (1, -1, A0), (1, -1, A1), (2, -1, A0), (2, -1, A1), (-1, 2, A0), (1, 2, A0), (2, 2, A0)]
ABOVE = [(0, 1, B1), (0, 1, B0), (0, 1, A1), (0, 1, A0), (0, 2, B1), (0, 2, A1), (-1, 1, A1), (-1, 1, A0),
         (1, 1, A1), (1, 1, A0), (2, 1, A1), (2, 1, A0), (-1, 2, A1), (1, 2, A1), (2, 2, A1)]
def device(x, y, z, c):
    return (lax.div(z, 4) * 4 + y, (x * 4 + lax.rem(z, 4)) * 2 + c)


HALVES = 2
HPAGES = PP // HALVES
NEAR = (0, 1, -1, 2)
COLS = {A0: (0, 512), A1: (512, 512), B0: (1024, 1152), B1: (2176, 1152)}
A_END, STRIP, AB_END = 1024, 2048, 3328
FIRST = {2: [(0, 0)], 4: [(-1, 0), (1, 0)], 5: [(0, -1), (0, 1)], 6: [(2, 0)], 7: [(0, 2)], 8: [(-1, -1)],
         10: [(1, -1), (-1, 1)], 11: [(1, 1)], 13: [(2, -1), (-1, 2)], 14: [(2, 1), (1, 2)], 15: [(2, 2)]}
FINISH = {2: [(0, 0)], 6: [(0, -1), (0, 1)], 8: [(-1, 0), (1, 0)], 9: [(0, 2), (2, 0)], 11: [(-1, -1)], 12: [(1, -1)],
          13: [(-1, 1), (1, 1)], 15: [(-1, 2), (1, 2)], 16: [(2, -1), (2, 1), (2, 2)]}
A_DONE = {2: [(-1, 0), (1, 0)], 4: [(0, -1), (0, 1)], 5: [(2, 0)], 6: [(0, 2)], 8: [(-1, -1), (-1, 1)], 10: [(1, -1), (1, 1)],
          12: [(2, -1), (2, 1)], 13: [(-1, 2)], 14: [(1, 2)], 15: [(2, 2)]}
B_DONE = {2: [(0, -1), (0, 1)], 4: [(-1, 0), (1, 0)], 5: [(0, 2)], 6: [(2, 0)], 8: [(-1, -1), (1, -1)], 10: [(-1, 1), (1, 1)],
          12: [(-1, 2), (1, 2)], 13: [(2, -1)], 14: [(2, 1)], 15: [(2, 2)]}
STRIPS = {4: [(0, -1), (0, 1)], 6: [(-1, 0), (1, 0)], 7: [(0, 2)], 8: [(2, 0)], 10: [(-1, -1), (1, -1)], 12: [(-1, 1), (1, 1)],
          14: [(-1, 2), (1, 2)], 15: [(2, -1)], 16: [(2, 1), (2, 2)]}
NEXT = {0: (1, 2, 3, 4), 1: (5,), 3: (6, 7), 4: (8,), 5: (9, 10), 6: (11,), 7: (12,), 8: (13,), 9: (14,), 11: (15,)}
HALVES = 2
HPAGES = PP // HALVES
NEAR = (0, 1, -1, 2)


def main_kernel(px_hbm, wd_hbm, gain_ref, rope_hbm, pool_ref, q_ref, len_ref, dest_ref, slot_in_ref, moe_hbm, ids_ref, ew_ref, w_hbm,
                att_ref, out_ref,
                px, wd_ref, tag_ref, esum, rope, rs_send, rs_recv, acc, zx_send, zx_recv, cache, pg_send, pg_recv, kv_send, kv_recv, kvbuf, q_recv, o_send,
                page_of, slot_of, src_of, rows, tags, wbuf, slot_ref, wt_ref,
                px_sem, wd_sem, strip_ssem, strip_rsem, rope_sem, rs_ssem, rs_rsem, zx_ssem, zx_rsem, pg_ssem, pg_rsem, kv_ssem, kv_rsem, q_ssem, q_rsem, o_ssem, o_rsem,
                load_sem, w_sem, ici_sem, pair_sem, recv_sem, recv2_sem, tag_send, tag_recv):
    pre, dec = lax.axis_index("pre"), lax.axis_index("dec")
    y = lax.rem(pre, 4)
    c = lax.rem(dec, 2)
    zl = lax.rem(lax.div(dec, 2), 4)
    x = lax.div(dec, 8)
    z = lax.div(pre, 4) * 4 + zl
    features = rows.shape[2]

    def chip(dx, dz):
        return lax.rem(x + dx + 4, 4) * 4 + lax.rem(z + dz + 8, 4)

    def peer(dx, dz, core):
        return device(lax.rem(x + dx + 4, 4), y, lax.rem(z + dz + 8, 8), core)

    def ypeer(dy):
        return device(x, lax.rem(y + dy, 4), z, c)

    def remote(src, dst, ssem, rsem, where):
        copy = pltpu.make_async_remote_copy(
            src_ref=src, dst_ref=dst, send_sem=ssem, recv_sem=rsem, device_id=where, device_id_type=MESH)
        copy.start()
        return copy

    def landed(ref, sem):
        pltpu.make_async_copy(ref, ref, sem).wait()

    def strip_from(dy):
        return pl.multiple_of(A_END * 3 + lax.rem(y - dy + 4, 4) * 256, 256)

    chunks = [(0, 0, 2048), (STRIP, strip_from(0), 256), (STRIP + 256, 2048, 1024)]
    chunks += [(AB_END + 256 * (dy - 1), strip_from(dy), 256) for dy in (1, 2, 3)]
    mine = pl.ds(pl.multiple_of(c * R_MOE, R_MOE), R_MOE)
    px_load = pltpu.make_async_copy(px_hbm, px, px_sem)
    px_load.start()
    wd_load = pltpu.make_async_copy(wd_hbm, wd_ref, wd_sem)
    wd_load.start()
    for to, of, size in chunks:
        pltpu.make_async_copy(moe_hbm.at[:, pl.ds(of, size)], rows.at[chip(0, 0), mine, pl.ds(to, size)], load_sem).start()
    barrier = pltpu.get_barrier_semaphore()
    greeted = 0
    for dx in (0, 1, 2, 3):
        for dz in (-2, -1, 0, 1, 2):
            for dc in (0, 1):
                if (dx, dz, dc) != (0, 0, 0):
                    pl.semaphore_signal(barrier, inc=1, device_id=peer(dx, dz, lax.rem(c + dc, 2)), device_id_type=MESH)
                    greeted += 1
    for dy in (1, 2, 3):
        pl.semaphore_signal(barrier, inc=1, device_id=ypeer(dy), device_id_type=MESH)
        greeted += 1
    pl.semaphore_signal(barrier, inc=1, device_id=peer(0, 4, c), device_id_type=MESH)
    greeted += 1

    rope_load = pltpu.make_async_copy(rope_hbm.at[:, y], rope, rope_sem)
    rope_load.start()
    for e in range(EXP_DEV):
        for t in range(2):
            for to, of, size in chunks:
                pltpu.make_async_copy(
                    w_hbm.at[e, t, pl.ds(of, size)], wbuf.at[pl.ds(to, size), pl.ds((e * 2 + t) * 128, 128)], w_sem.at[e * 2 + t]).start()
    i0 = lax.broadcasted_iota(jnp.int32, (R_MOE, 128), 0)
    i1 = lax.broadcasted_iota(jnp.int32, (R_MOE, 128), 1)
    spread_rows = jnp.where(i1 == i0 + c * R_MOE, 1.0, 0.0).astype(jnp.bfloat16)
    tag_rows = [
        jnp.dot(part, spread_rows, preferred_element_type=jnp.float32)
        for part in (ids_ref[...].astype(jnp.float32).astype(jnp.bfloat16), ew_ref[...])
    ]
    tag_ref[...] = jnp.concatenate(tag_rows, axis=0).astype(jnp.bfloat16)
    tags[dec] = tag_ref[...]

    px_load.wait()
    wd_load.wait()
    for h in range(HALVES):
        for dy in (2, 1, 3, 0):
            yy = lax.rem(y + dy, 4)
            lhs = px[pl.ds(h * HPAGES, HPAGES), yy].reshape(HPAGES * 16, px.shape[3])
            part = lax.dot_general(lhs, wd_ref[...], (((1,), (1,)), ((), ())), preferred_element_type=jnp.float32)
            if dy:
                rs_send[dy - 1, h] = part.astype(jnp.bfloat16)
            else:
                acc[h] = part
    pl.semaphore_wait(barrier, greeted)
    rs_copies = []
    for h in range(HALVES):
        for dy in (2, 1, 3):
            rs_copies.append(remote(rs_send.at[dy - 1, h], rs_recv.at[dy - 1, h], rs_ssem.at[dy - 1, h], rs_rsem.at[dy - 1, h], ypeer(dy)))

    def block(dx, dz, core, first, size):
        return rows.at[chip(dx, dz), pl.ds(pl.multiple_of(core * R_MOE, R_MOE), R_MOE), pl.ds(first, size)]

    def push(dx, dz, q, sx, sz):
        part = block(dx, dz, c, *COLS[q])
        remote(part, part, ici_sem, recv_sem.at[chip(dx, dz), q], peer(sx, sz, c))

    def push_next(step):
        for n in NEXT.get(step, ()):
            dx, dz, q = LEFT[n - 1]
            push(dx + 1, dz, q, 1, 0)
            dx, dz, q = BELOW[n - 1]
            push(dx, dz + 1, q, 0, 1)
            dx, dz, q = RIGHT[n - 1]
            push(dx - 1, dz, q, -1, 0)
            dx, dz, q = ABOVE[n - 1]
            push(dx, dz - 1, q, 0, -1)

    SPANS = [(0, A_END), (A_END, AB_END - A_END), (AB_END, features - AB_END)]

    def share(dx, dz, span):
        part = block(dx, dz, c, *SPANS[span])
        remote(part, part, pair_sem, recv2_sem.at[chip(dx, dz), span], peer(0, 0, 1 - c))

    def shared(dx, dz, span):
        landed(block(dx, dz, 1 - c, *SPANS[span]), recv2_sem.at[chip(dx, dz), span])

    def send_strips(dx, dz):
        for dy in (1, 2, 3):
            remote(block(dx, dz, c, STRIP, 256), block(dx, dz, c, AB_END + 256 * (dy - 1), 256), strip_ssem,
                   strip_rsem.at[chip(dx, dz), dy - 1], ypeer(dy))

    def wait_strips(dx, dz):
        for dy in (1, 2, 3):
            landed(block(dx, dz, c, AB_END + 256 * (dy - 1), 256), strip_rsem.at[chip(dx, dz), dy - 1])
        share(dx, dz, 2)

    landed(block(0, 0, c, 0, features), load_sem)
    push_next(0)

    for span in range(3):
        share(0, 0, span)
    tag_copies = []
    for dx in (0, 1, 2, 3):
        for dz in NEAR:
            for dc in (0, 1):
                if (dx, dz, dc) != (0, 0, 0):
                    n = len(tag_copies)
                    tag_copies.append(remote(tag_ref, tags.at[dec], tag_send.at[n], tag_recv.at[dec], peer(dx, dz, lax.rem(c + dc, 2))))
    q_copies = []
    for dy in (1, 2, 3):
        yy = lax.rem(y + dy, 4)
        q_copies.append(remote(q_ref.at[yy], q_recv.at[y], q_ssem.at[dy - 1], q_rsem.at[y], ypeer(dy)))
    q_recv[y] = q_ref[y]

    def read_tables():
        dests = [dest_ref[dec * PP + p] for p in range(PP)]

        def find_page(d, carry):
            found = jnp.int32(0)
            for p in range(PP):
                found = jnp.where(dests[p] == d, p, found)
            page_of[d] = found
            return carry

        lax.fori_loop(0, 32, find_page, 0)

        def find_slot(s, carry):
            found = jnp.int32(-1)
            for p in range(PP):
                found = jnp.where(dest_ref[s * PP + p] == dec, slot_in_ref[s * PP + p], found)
            slot_of[s] = found
            return carry

        lax.fori_loop(0, 32, find_slot, 0)

        def find_source(k, carry):
            found = jnp.int32(-1)
            for s in range(32):
                found = jnp.where(slot_of[s] == k, s, found)
            src_of[k] = found
            return carry

        lax.fori_loop(0, SLOTS, find_source, 0)


    def read_tags():
        for dx in (0, 1, 2, 3):
            for dz in NEAR:
                for dc in (0, 1):
                    if (dx, dz, dc) != (0, 0, 0):
                        s = 2 * chip(dx, dz) + lax.rem(c + dc, 2)
                        landed(tags.at[s], tag_recv.at[s])
        both = tags[...].astype(jnp.float32).reshape(16, 2, 16, 128)
        both = both[:, 0] + both[:, 1]
        ids, weights = both[:, :8], both[:, 8:]
        i0 = lax.broadcasted_iota(jnp.int32, (128, 128), 0)
        i1 = lax.broadcasted_iota(jnp.int32, (128, 128), 1)
        earlier = ((i0 < i1) & (lax.div(i0, 64) == lax.div(i1, 64))).astype(jnp.float32).astype(jnp.bfloat16)
        shift = jnp.where(lax.broadcasted_iota(jnp.int32, (16, 128), 1) >= 64, 8.0, 0.0)
        for e in range(EXP_DEV):
            hit = ids == (dec * EXP_DEV + e).astype(jnp.float32)
            member = jnp.sum(jnp.where(hit, 1.0, 0.0), axis=1)
            wt_ref[e] = jnp.sum(jnp.where(hit, weights, 0.0), axis=1)
            rank = jnp.dot(member.astype(jnp.bfloat16), earlier, preferred_element_type=jnp.float32)
            slot_ref[e] = jnp.where(member > 0.5, rank + shift, -1.0)

    def first_product(dx, dz):
        shared(dx, dz, 0)
        shared(dx, dz, 1)
        k = chip(dx, dz)
        esum[k] = jnp.dot(rows[k, :, :AB_END], wbuf[:AB_END], preferred_element_type=jnp.float32)

    def finish_product(dx, dz):
        shared(dx, dz, 2)
        k = chip(dx, dz)
        i0 = lax.broadcasted_iota(jnp.int32, (128, 128), 0)
        i1 = lax.broadcasted_iota(jnp.int32, (128, 128), 1)
        place = lax.broadcasted_iota(jnp.int32, (16, 128), 0).astype(jnp.float32)
        both = esum[k] + jnp.dot(rows[k, :, AB_END:], wbuf[AB_END:], preferred_element_type=jnp.float32)
        for e in range(EXP_DEV):
            gate, up = both[:, e * 256:e * 256 + 128], both[:, e * 256 + 128:e * 256 + 256]
            wrow = wt_ref[e, pl.ds(k, 1), :]
            spread = jnp.where(i0 == i1, jnp.broadcast_to(wrow, (128, 128)), 0.0).astype(jnp.bfloat16)
            wcol = jnp.dot(spread, jnp.ones((128, 128), jnp.bfloat16), preferred_element_type=jnp.float32)
            hidden = (gate / (1.0 + jnp.exp(-gate)) * up * wcol).astype(jnp.bfloat16)
            srow = slot_ref[e, pl.ds(k, 1), :]
            choose = jnp.where(jnp.broadcast_to(srow, (16, 128)) == place, 1.0, 0.0).astype(jnp.bfloat16)
            out_ref[e, pl.ds(pl.multiple_of(k * 16, 16), 16), :] = jnp.dot(
                choose, hidden, preferred_element_type=jnp.float32).astype(jnp.bfloat16)

    zx_copies, pg_copies, kv_copies, o_copies = [], [], [], []

    def add_y(h):
        total = acc[h]
        for dy in (1, 2, 3):
            landed(rs_recv.at[dy - 1, h], rs_rsem.at[dy - 1, h])
            total = total + rs_recv[dy - 1, h].astype(jnp.float32)
        acc[h] = total
        zx_send[h] = total.astype(jnp.bfloat16)
        zx_copies.append(remote(zx_send.at[h], zx_recv.at[h], zx_ssem.at[h], zx_rsem.at[h], peer(0, 4, c)))

    def finish_cache(h):
        landed(zx_recv.at[h], zx_rsem.at[h])
        if h == 0:
            rope_load.wait()
        total = acc[h] + zx_recv[h].astype(jnp.float32)
        lat, turn = total[:, :KVL], total[:, KVL:]
        normed = lat * lax.rsqrt(jnp.mean(lat * lat, axis=1, keepdims=True) + NORM_EPSILON) * gain_ref[...]
        table = rope[pl.ds(h * HPAGES, HPAGES)].reshape(HPAGES * 16, 128)
        swapped = jnp.concatenate([turn[:, 32:], turn[:, :32]], axis=1)
        turned = turn * table[:, :64] + swapped * table[:, 64:]
        done = jnp.concatenate([normed, turned], axis=1).astype(jnp.bfloat16)
        cache[pl.ds(h * HPAGES, HPAGES)] = done.reshape(HPAGES, 16, LAT)

    def send_pages():
        n = 0
        for dx in (0, 1, 2, 3):
            for dz in NEAR:
                for dc in (0, 1):
                    cc = lax.rem(c + dc, 2)
                    page = cache[page_of[2 * chip(dx, dz) + cc]]
                    if (dx, dz, dc) == (0, 0, 0):
                        pg_recv[dec] = page
                        continue
                    pg_send[n] = page
                    pg_copies.append(remote(pg_send.at[n], pg_recv.at[dec], pg_ssem.at[n], pg_rsem.at[dec], peer(dx, dz, cc)))
                    n += 1

    def place_pages():
        for dx in (0, 1, 2, 3):
            for dz in NEAR:
                for dc in (0, 1):
                    if (dx, dz, dc) != (0, 0, 0):
                        s = 2 * chip(dx, dz) + lax.rem(c + dc, 2)
                        landed(pg_recv.at[s], pg_rsem.at[s])
        for k in range(SLOTS):
            kv_send[k // 8, k % 8] = pg_recv[jnp.maximum(src_of[k], 0)]
        for dy in (1, 2, 3):
            yy = lax.rem(y + dy, 4)
            kv_copies.append(remote(kv_send.at[yy], kv_recv.at[y], kv_ssem.at[dy - 1], kv_rsem.at[y], ypeer(dy)))
        kv_recv[y] = kv_send[y]

    def attend():
        for dy in (1, 2, 3):
            yy = lax.rem(y + dy, 4)
            landed(kv_recv.at[yy], kv_rsem.at[yy])
            landed(q_recv.at[yy], q_rsem.at[yy])
        for k in range(8):
            fresh = src_of[y * 8 + k] >= 0
            for yy in range(4):
                kvbuf[k // 4, yy, k % 4] = jnp.where(fresh, kv_recv[yy, k], pool_ref[k, yy])
        col = lax.broadcasted_iota(jnp.int32, (64, 256), 1)
        at = lax.rem(lax.div(col, 16), 4) * PAGE + lax.div(col, 64) * 16 + lax.rem(col, 16)
        for rr in range(2):
            kv = kvbuf[rr].reshape(PAGES_ROW * PAGE, LAT)
            query = q_recv[:, rr].reshape(64, LAT)
            scores = lax.dot_general(query, kv, (((1,), (1,)), ((), ())), preferred_element_type=jnp.float32) * HEAD_QK ** (-0.5)
            masked = jnp.where(at < len_ref[2 * y + rr], scores, -jnp.inf)
            raw = jnp.exp(masked - jnp.max(masked, axis=1, keepdims=True))
            probs = (raw / jnp.sum(raw, axis=1, keepdims=True)).astype(jnp.bfloat16)
            got = jnp.dot(probs, kv[:, :KVL], preferred_element_type=jnp.float32).astype(jnp.bfloat16)
            o_send[:, rr] = got.reshape(4, 16, KVL)
        for dy in (1, 2, 3):
            yy = lax.rem(y + dy, 4)
            o_copies.append(remote(o_send.at[yy], att_ref.at[y], o_ssem.at[dy - 1], o_rsem.at[y], ypeer(dy)))
        att_ref[y] = o_send[y]

    events = {1: [read_tables], 2: [lambda: add_y(0)], 4: [lambda: add_y(1)], 5: [lambda: finish_cache(0)],
              7: [lambda: finish_cache(1), send_pages], 11: [place_pages], 15: [attend]}

    for n in range(1, 17):
        if n <= 15:
            for plan in (LEFT, RIGHT, BELOW, ABOVE):
                dx, dz, q = plan[n - 1]
                landed(block(dx, dz, c, *COLS[q]), recv_sem.at[chip(dx, dz), q])
            push_next(n)
        for item in B_DONE.get(n, []):
            send_strips(*item)
            share(*item, 1)
        for item in A_DONE.get(n, []):
            share(*item, 0)
        for item in STRIPS.get(n, []):
            wait_strips(*item)
        if n == 2:
            read_tags()
            for i in range(2 * EXP_DEV):
                landed(wbuf.at[:, pl.ds(i * 128, 128)], w_sem.at[i])
        for event in events.get(n, []):
            event()
        for item in FIRST.get(n, []):
            first_product(*item)
        for item in FINISH.get(n, []):
            finish_product(*item)

    for dy in (1, 2, 3):
        yy = lax.rem(y + dy, 4)
        landed(att_ref.at[yy], o_rsem.at[yy])
    landed(rows.at[pl.ds(0, 8)], pair_sem)
    landed(rows.at[pl.ds(0, 15), pl.ds(0, R_MOE), pl.ds(0, AB_END)], ici_sem)
    landed(rows.at[pl.ds(0, 15), pl.ds(0, R_MOE), pl.ds(AB_END, features - AB_END)], strip_ssem)
    for copy in tag_copies + q_copies + rs_copies + zx_copies + pg_copies + kv_copies + o_copies:
        copy.wait_send()


def rope_table():
    place = np.arange(P_TOK, dtype=np.float32)[:, None]
    angle = (place * (10000.0 ** (-2.0 * np.arange(32, dtype=np.float64) / 64)).astype(np.float32)[None, :]).astype(np.float64)
    cosine, sine = np.cos(angle), np.sin(angle)
    return np.concatenate([cosine, cosine, -sine, sine], axis=1).astype(np.float32)


def shards(
    prompt_x,
    w_dkv,
    kv_gain,
    cache_pool,
    queries,
    row_lengths,
    page_dest,
    page_slot,
    moe_x,
    expert_ids,
    expert_weights,
    w_gate_up,
):
    y = lax.rem(lax.axis_index("pre"), 4)
    features = moe_x.shape[1]
    part = prompt_x.shape[1]
    px = prompt_x.reshape(PP, 4, 16, part)
    rope = jnp.asarray(rope_table()).reshape(PP, 4, 16, 128)
    pool = lax.dynamic_slice_in_dim(cache_pool, y * 8, 8, 0).reshape(8, 4, 16, LAT)
    heads = queries.shape[1] // LAT
    q = queries.reshape(4, 2, heads, LAT)
    vmem = pl.BlockSpec(memory_space=pltpu.VMEM)
    smem = pl.BlockSpec(memory_space=pltpu.SMEM)
    hbm = pl.BlockSpec(memory_space=pl.ANY)
    dma = pltpu.SemaphoreType.DMA
    bf = jnp.bfloat16
    att, out = pl.pallas_call(
        main_kernel,
        out_shape=(jax.ShapeDtypeStruct((4, 2, heads, KVL), bf), jax.ShapeDtypeStruct((EXP_DEV, 256, 128), bf)),
        in_specs=[hbm, hbm, vmem, hbm, vmem, vmem, smem, smem, smem, hbm, vmem, vmem, hbm],
        out_specs=(vmem, vmem),
        scratch_shapes=[
            pltpu.VMEM((PP, 4, 16, part), bf),
            pltpu.VMEM((LAT, part), bf),
            pltpu.VMEM((16, 128), bf),
            pltpu.VMEM((16, 2 * R_MOE, EXP_DEV * 256), jnp.float32),
            pltpu.VMEM((PP, 16, 128), jnp.float32),
            pltpu.VMEM((3, HALVES, HPAGES * 16, LAT), bf),
            pltpu.VMEM((3, HALVES, HPAGES * 16, LAT), bf),
            pltpu.VMEM((HALVES, HPAGES * 16, LAT), jnp.float32),
            pltpu.VMEM((HALVES, HPAGES * 16, LAT), bf),
            pltpu.VMEM((HALVES, HPAGES * 16, LAT), bf),
            pltpu.VMEM((PP, 16, LAT), bf),
            pltpu.VMEM((31, 16, LAT), bf),
            pltpu.VMEM((32, 16, LAT), bf),
            pltpu.VMEM((4, 8, 16, LAT), bf),
            pltpu.VMEM((4, 8, 16, LAT), bf),
            pltpu.VMEM((2, 4, 4, 16, LAT), bf),
            pltpu.VMEM((4, 2, heads, LAT), bf),
            pltpu.VMEM((4, 2, heads, KVL), bf),
            pltpu.SMEM((32,), jnp.int32),
            pltpu.SMEM((32,), jnp.int32),
            pltpu.SMEM((32,), jnp.int32),
            pltpu.VMEM((16, 2 * R_MOE, features), bf),
            pltpu.VMEM((32, 16, 128), bf),
            pltpu.VMEM((features, EXP_DEV * 256), bf),
            pltpu.VMEM((EXP_DEV, 16, 128), jnp.float32),
            pltpu.VMEM((EXP_DEV, 16, 128), jnp.float32),
            dma, dma, dma, dma((16, 3)), dma, dma((3, HALVES)), dma((3, HALVES)), dma((HALVES,)), dma((HALVES,)), dma((31,)), dma((32,)),
            dma((3,)), dma((4,)), dma((3,)), dma((4,)), dma((3,)), dma((4,)),
            dma, dma((8,)), dma, dma, dma((16, 4)), dma((16, 3)), dma((31,)), dma((32,)),
        ],
        compiler_params=pltpu.CompilerParams(collective_id=0, has_side_effects=True, vmem_limit_bytes=58 * 1024 * 1024),
    )(px, w_dkv.T, kv_gain.reshape(1, KVL), rope, pool, q, row_lengths, page_dest, page_slot, moe_x, expert_ids.T, expert_weights.T, w_gate_up)
    return (att.reshape(R_ATT, heads * KVL), out)


def solution(mesh):
    return jax.shard_map(
        shards,
        mesh=mesh,
        in_specs=(
            P("dec", "pre"),
            P("pre", None),
            P(),
            P("dec", None),
            P("dec", "pre"),
            P("dec"),
            P(),
            P(),
            P("dec", None),
            P("dec", None),
            P("dec", None),
            P("dec", None, None, "pre"),
        ),
        out_specs=(P("dec", "pre"), P("dec", None, "pre")),
        check_vma=False,
    )
```
